32 devices in a mesh: grp: 4 (over y, x), ctx: 8 (over z, core).
Axes of the slice: x: 2, y: 2, z: 4, core: 2. Of those that a mesh axis runs over, the one named last changes fastest.
Arguments:
- query_raw: bfloat16 [8192, 256], P(('grp', 'ctx')), may hold values from -6 to 6
- key_raw: bfloat16 [8192, 256], P(('grp', 'ctx')), may hold values from -6 to 6
- values: bfloat16 [8192, 256], P(('grp', 'ctx')), may hold values from -6 to 6
- band_reach: int32 [64], P(('grp', 'ctx')), may hold values from 1 to 2, as said below
- partners: int32 [64, 4], P(('grp', 'ctx')), may hold values from 0 to 63, as said below
- gain_query: float32 [2, 128], replicated, may hold values from 0.5 to 2
- gain_key: float32 [2, 128], replicated, may hold values from 0.5 to 2
- cotangent: bfloat16 [8192, 256], P(('grp', 'ctx')), may hold values from -6 to 6
Outputs:
- output: bfloat16 [8192, 256], P(('grp', 'ctx'))
- grad_query: bfloat16 [8192, 256], P(('grp', 'ctx'))
- grad_key: bfloat16 [8192, 256], P(('grp', 'ctx'))
- grad_value: bfloat16 [8192, 256], P(('grp', 'ctx'))
The draws below stay inside these ranges and needn't reach their ends.
Inputs may be any that keep to these rules, and one draw needn't show every extreme that they name: `band_reach`: some query block has reach 2. partners[b, l] is a block of the device whose index is (b // 2) xor (32 // 2**(l+1)).
All inputs are finite; a program needn't handle non-finite values.
Results may differ from the reference program's by a relative error of at most 0.0099.
Values may be sent and summed in bfloat16 or wider, within the bound.
A program may use at most 64 MiB of HBM per device.

```python
import math
import jax
import jax.numpy as jnp
from jax import lax

HEADS = 2
HEAD_DIM = 128
BLOCK = 128
BAND = 2
LEVELS = 4
SHARDS = 32
TOKENS = 8192
BLOCKS_DEV = 2
BLOCKS = 64


def draw_band_reach(key, part):
    reach = jax.random.randint(key, (BLOCKS,), 1, BAND + 1)
    places = jnp.arange(BLOCKS)
    reach = jnp.where(places == 0, 1, reach)
    reach = jnp.where(places == 1, BAND, reach)
    return reach.astype(jnp.int32)


def draw_partners(key, part):
    block_ids = jnp.arange(BLOCKS, dtype=jnp.int32)[:, None]
    level_ids = jnp.arange(LEVELS, dtype=jnp.int32)[None, :]
    distance = jnp.right_shift(jnp.int32(SHARDS), level_ids + 1)
    owner = block_ids // BLOCKS_DEV
    partner_device = jnp.bitwise_xor(owner, distance)
    picked = jax.random.randint(key, (BLOCKS, LEVELS), 0, BLOCKS_DEV)
    picked = jnp.where(owner == SHARDS // 2 - 1, BLOCKS_DEV - 1, picked)
    picked = jnp.where(owner == SHARDS // 2, 0, picked)
    return (partner_device * BLOCKS_DEV + picked).astype(jnp.int32)


def steps_of(rng, extent, cuts, smallest, high):
    def one(axis_at, parts):
        draws = jax.random.uniform(jax.random.fold_in(jax.random.fold_in(rng, 6), axis_at), (parts,), jnp.float32, smallest / len(cuts), high / len(cuts))
        return jnp.repeat(jnp.exp(draws), extent[axis_at] // parts).reshape((-1,) + (1,) * (len(extent) - axis_at - 1))

    level = one(*cuts[0])
    for cut in cuts[1:]:
        level = level * one(*cut)
    return level


def bell_draw(rng, dims, width, most, shards=(), kind=jnp.bfloat16):
    array = width * jax.random.normal(rng, dims, jnp.float32)
    if shards:
        array = array * steps_of(rng, dims, shards, -0.22, 0.18)
    return jnp.clip(array, -most, most).astype(kind)


def setup_inputs(seed: int = 0) -> dict:
    keys = jax.random.split(jax.random.key(seed), 9)
    return {
        "query_raw": bell_draw(keys[0], (TOKENS, HEADS * HEAD_DIM), 1.0, 6.0, ((0, 32),)),
        "key_raw": bell_draw(keys[1], (TOKENS, HEADS * HEAD_DIM), 1.0, 6.0, ((0, 32),)),
        "values": bell_draw(keys[2], (TOKENS, HEADS * HEAD_DIM), 1.0, 6.0, ((0, 32),)),
        "band_reach": draw_band_reach(jax.random.fold_in(keys[8], 71), 0),
        "partners": draw_partners(jax.random.fold_in(keys[8], 71), 0),
        "gain_query": jnp.clip(jnp.exp(jax.random.uniform(keys[5], (HEADS, HEAD_DIM), jnp.float32, math.log(0.5), math.log(2.0))), 0.5, 2.0),
        "gain_key": jnp.clip(jnp.exp(jax.random.uniform(keys[6], (HEADS, HEAD_DIM), jnp.float32, math.log(0.5), math.log(2.0))), 0.5, 2.0),
        "cotangent": bell_draw(keys[7], (TOKENS, HEADS * HEAD_DIM), 1.0, 6.0, ((0, 32),)),
    }


epsilon = 1e-05

def layer_norm(inputs, gain_row):
    average = lax.optimization_barrier(jnp.mean(inputs, axis=-1, keepdims=True))
    centred = inputs - average
    inverse = lax.rsqrt(lax.optimization_barrier(jnp.mean(centred * centred, axis=-1, keepdims=True)) + epsilon)
    normed = centred * inverse
    return (normed, inverse, normed * gain_row)

def norm_back(upstream, normed, inverse, gain_row):
    scaled = upstream * gain_row
    first = lax.optimization_barrier(jnp.mean(scaled, axis=-1, keepdims=True))
    second = lax.optimization_barrier(jnp.mean(scaled * normed, axis=-1, keepdims=True))
    return (scaled - first - normed * second) * inverse

def reference(query_raw, key_raw, values, band_reach, partners, gain_query, gain_key, cotangent):
    tokens, row_width = query_raw.shape
    head_dim = row_width // HEADS
    block_count = tokens // BLOCK
    score_scale = head_dim ** (-0.5)
    q_normed, q_inverse, q_scaled = layer_norm(query_raw.astype(jnp.float32).reshape(tokens, HEADS, head_dim), gain_query)
    k_normed, k_inverse, k_scaled = layer_norm(key_raw.astype(jnp.float32).reshape(tokens, HEADS, head_dim), gain_key)
    query_low = q_scaled.astype(jnp.bfloat16).reshape(block_count, BLOCK, HEADS, head_dim)
    key_low = k_scaled.astype(jnp.bfloat16).reshape(block_count, BLOCK, HEADS, head_dim)
    value_blocks = values.reshape(block_count, BLOCK, HEADS, head_dim)
    grad_blocks = cotangent.reshape(block_count, BLOCK, HEADS, head_dim)
    offsets = jnp.arange(2 * BAND + 1, dtype=jnp.int32) - BAND

    def block_step(totals, block_index):
        key_acc, value_acc = totals
        target = block_index + offsets
        band_ok = (jnp.abs(offsets) <= band_reach[block_index]) & (target >= 0) & (target < block_count)
        chosen = jnp.concatenate((jnp.clip(target, 0, block_count - 1).astype(jnp.int32), partners[block_index].astype(jnp.int32)))
        usable = jnp.concatenate((band_ok, jnp.ones((LEVELS,), dtype=jnp.bool_)))
        key_set = key_low[chosen].astype(jnp.float32)
        value_set = value_blocks[chosen].astype(jnp.float32)
        query_block = query_low[block_index].astype(jnp.float32)
        grad_block = grad_blocks[block_index].astype(jnp.float32)
        scores = jnp.einsum('qhd,jkhd->hqjk', query_block, key_set) * score_scale
        allowed = usable[None, None, :, None]
        row_total = lax.optimization_barrier(jnp.sum(jnp.where(allowed, jnp.exp(scores), 0.0), axis=(2, 3)))
        log_total = jnp.log(row_total)
        probability = jnp.where(allowed, jnp.exp(scores - log_total[:, :, None, None]), 0.0)
        attention_weight = lax.optimization_barrier(probability.astype(jnp.bfloat16)).astype(jnp.float32)
        output = jnp.einsum('hqjk,jkhd->qhd', attention_weight, value_set).astype(jnp.bfloat16)
        row_delta = lax.optimization_barrier(jnp.sum(grad_block * output.astype(jnp.float32), axis=-1))
        grad_prob = jnp.einsum('qhd,jkhd->hqjk', grad_block, value_set)
        score_gradient = probability * (grad_prob - jnp.transpose(row_delta)[:, :, None, None])
        score_gradient = lax.optimization_barrier(score_gradient.astype(jnp.bfloat16)).astype(jnp.float32)
        grad_qnorm = jnp.einsum('hqjk,jkhd->qhd', score_gradient, key_set) * score_scale
        key_terms = jnp.einsum('hqjk,qhd->jkhd', score_gradient, query_block) * score_scale
        value_terms = jnp.einsum('hqjk,qhd->jkhd', attention_weight, grad_block)
        key_acc = key_acc.at[chosen].add(key_terms)
        value_acc = value_acc.at[chosen].add(value_terms)
        return ((key_acc, value_acc), (output, grad_qnorm))
    empty = jnp.zeros((block_count, BLOCK, HEADS, head_dim), jnp.float32)
    (key_acc, value_acc), (outputs, grad_qnorms) = lax.scan(block_step, (empty, empty), jnp.arange(block_count, dtype=jnp.int32))
    output = outputs.reshape(tokens, row_width)
    grad_query = norm_back(grad_qnorms.reshape(tokens, HEADS, head_dim), q_normed, q_inverse, gain_query)
    grad_key = norm_back(key_acc.reshape(tokens, HEADS, head_dim), k_normed, k_inverse, gain_key)
    grad_value = value_acc.astype(jnp.bfloat16).reshape(tokens, row_width)
    return (output, grad_query.astype(jnp.bfloat16).reshape(tokens, row_width), grad_key.astype(jnp.bfloat16).reshape(tokens, row_width), grad_value)
```

```python
import functools
import math

import jax
import jax.numpy as jnp
from jax import lax
from jax.experimental import pallas as pl
from jax.experimental.pallas import tpu as pltpu
from jax.sharding import PartitionSpec as P

HEADS = 2
BLOCK = 128
LEVELS = 4
BAND = 2
EPS = 1e-05
AXES = ("grp", "ctx")
MESH = pl.DeviceIdType.MESH
F32 = jnp.float32
BF16 = jnp.bfloat16
LEFT, RIGHT = 0, 1
SLOTS = 2 + LEVELS
KEY, VAL, QRY, COT, STAT = 0, 1, 2, 3, 4
POS = 2 * BAND + 1 + LEVELS


def dot_t(a, b):
    return lax.dot_general(a, b, (((1,), (1,)), ((), ())), preferred_element_type=F32)


def dot_n(a, b):
    return jnp.dot(a, b, preferred_element_type=F32)


def rows(block):
    return pl.ds(block * BLOCK, BLOCK)


def kernel(
    shards,
    inner,
    q_ref,
    k_ref,
    v_ref,
    g_ref,
    gq_ref,
    gk_ref,
    reach_ref,
    part_ref,
    o_ref,
    dq_ref,
    dk_ref,
    dv_ref,
    buf,
    stat,
    own_stat,
    out_stat,
    qn,
    kn,
    qhat,
    khat,
    qinv,
    kinv,
    kcat,
    vcat,
    e_s,
    g_s,
    dk_acc,
    dv_acc,
    send_sem,
    recv_sem,
    fwd_sem,
):
    me = lax.axis_index(AXES)
    hd = gq_ref.shape[1]
    scale = hd ** (-0.5)
    log2e_scale = scale * math.log2(math.e)
    masks = [shards >> (level + 1) for level in range(LEVELS)]
    relay = 2 in masks
    near = 2 + masks.index(2) if relay else None
    has_left = me > 0
    has_right = me < shards - 1
    core = lax.rem(me, 2)
    chip_odd = lax.rem(me // 2, 2)
    peers = [jnp.bitwise_xor(me, m) for m in masks]

    def at(t):
        return (t // inner, lax.rem(t, inner))

    barrier = pltpu.get_barrier_semaphore()
    for t in peers:
        pl.semaphore_signal(barrier, inc=1, device_id=at(t), device_id_type=MESH)

    @pl.when(has_left)
    def _():
        pl.semaphore_signal(barrier, inc=1, device_id=at(me - 1), device_id_type=MESH)

    @pl.when(has_right)
    def _():
        pl.semaphore_signal(barrier, inc=1, device_id=at(me + 1), device_id_type=MESH)

    pl.semaphore_wait(
        barrier, LEVELS + has_left.astype(jnp.int32) + has_right.astype(jnp.int32)
    )

    sources = {KEY: kn, VAL: v_ref, QRY: qn, COT: g_ref}

    def copy(slot, what, t):
        if what == STAT:
            src, dst = out_stat.at[slot], stat.at[slot]
        else:
            src, dst = sources[what], buf.at[slot, what]
        return pltpu.make_async_remote_copy(
            src_ref=src,
            dst_ref=dst,
            send_sem=send_sem.at[slot, what],
            recv_sem=recv_sem.at[slot, what],
            device_id=at(t),
            device_id_type=MESH,
        )

    def forward(slot, what, t):
        return pltpu.make_async_remote_copy(
            src_ref=buf.at[near, what],
            dst_ref=buf.at[slot, what],
            send_sem=fwd_sem.at[what],
            recv_sem=recv_sem.at[slot, what],
            device_id=at(t),
            device_id_type=MESH,
        )

    def to_right(what):
        if relay and what != STAT:
            return has_right & ((core == 0) | (chip_odd == 1))
        return has_right

    def to_left(what):
        if relay and what != STAT:
            return has_left & ((core == 1) | (chip_odd == 0))
        return has_left

    def each_copy(what, act):
        for level in reversed(range(LEVELS)):
            act(copy(2 + level, what, peers[level]))

        @pl.when(to_right(what))
        def _():
            act(copy(LEFT, what, me + 1))

        @pl.when(to_left(what))
        def _():
            act(copy(RIGHT, what, me - 1))

    def send(what):
        each_copy(what, lambda c: c.start())

    def arrived(slot, what):
        if slot == LEFT:

            @pl.when(has_left)
            def _():
                copy(LEFT, what, me - 1).wait_recv()
        elif slot == RIGHT:

            @pl.when(has_right)
            def _():
                copy(RIGHT, what, me + 1).wait_recv()
        else:
            copy(slot, what, peers[slot - 2]).wait_recv()

    def each_forward(what, act):
        if not relay:
            return

        @pl.when((core == 0) & (chip_odd == 0))
        def _():
            act(forward(RIGHT, what, me + 1))

        @pl.when((core == 1) & (chip_odd == 1))
        def _():
            act(forward(LEFT, what, me - 1))

    send(VAL)

    def normalize(x_ref, gain_ref, hat_ref, inv_ref, out_ref):
        for h in range(HEADS):
            cols = slice(h * hd, (h + 1) * hd)
            x = x_ref[:, cols].astype(F32)
            x = x - jnp.mean(x, axis=-1, keepdims=True)
            inv = lax.rsqrt(jnp.mean(x * x, axis=-1, keepdims=True) + EPS)
            hat = x * inv
            hat_ref[:, cols] = hat
            inv_ref[:, cols] = jnp.broadcast_to(inv, hat.shape)
            out_ref[:, cols] = (hat * gain_ref[h : h + 1, :]).astype(BF16)

    normalize(k_ref, gk_ref, khat, kinv, kn)
    send(KEY)
    normalize(q_ref, gq_ref, qhat, qinv, qn)
    send(QRY)
    send(COT)

    for slot, missing in ((LEFT, me == 0), (RIGHT, me == shards - 1)):

        @pl.when(missing)
        def _():
            for what in (KEY, VAL, QRY, COT):
                buf[slot, what] = jnp.zeros(buf.shape[2:], BF16)
            stat[slot] = jnp.zeros(stat.shape[1:], F32)

    def head(h):
        return pl.ds(pl.multiple_of(h * hd, hd), hd)

    reach = [reach_ref[b] for b in range(2)]
    picks = [[part_ref[b, lv] - peers[lv] * 2 for lv in range(LEVELS)] for b in range(2)]

    def one(flag):
        return jnp.where(flag, 1.0, 0.0).astype(F32)

    left_ok, right_ok = one(has_left), one(has_right)

    def score(b, first, count, weights):
        span = pl.ds(first * BLOCK, count * BLOCK)

        def body(h, carry):
            s = dot_t(qn[rows(b), head(h)], kcat[b, span, head(h)])
            gp = dot_t(g_ref[rows(b), head(h)], vcat[b, span, head(h)])
            e = jnp.exp2(s * log2e_scale)
            for i in range(count):
                w = weights[i]
                part = e[:, i * BLOCK : (i + 1) * BLOCK]
                if w is not None:
                    part = part * w
                e_s[2 * b + h, :, rows(first + i)] = part
            g_s[2 * b + h, :, span] = gp
            return carry

        lax.fori_loop(0, HEADS, body, 0)

    def place(b, pos, key, val):
        kcat[b, rows(pos), :] = key
        vcat[b, rows(pos), :] = val

    for b in range(2):
        for c in range(2):
            place(b, 2 - b + c, kn[rows(c), :], v_ref[rows(c), :])
        score(b, 2 - b, 2, [None if c == b else one(reach[b] >= 1) for c in range(2)])

    def blend(m, first, second):
        return (first.astype(F32) * (1.0 - m) + second.astype(F32) * m).astype(BF16)

    def partner_scores(level):
        slot = 2 + level
        arrived(slot, VAL)
        if slot == near:
            each_forward(VAL, lambda c: c.start())
        arrived(slot, KEY)
        if slot == near:
            each_forward(KEY, lambda c: c.start())
        for b in range(2):
            m = picks[b][level].astype(F32)
            place(
                b,
                2 * BAND + 1 + level,
                blend(m, buf[slot, KEY, rows(0), :], buf[slot, KEY, rows(1), :]),
                blend(m, buf[slot, VAL, rows(0), :], buf[slot, VAL, rows(1), :]),
            )
            score(b, 2 * BAND + 1 + level, 1, [None])

    partner_scores(0)
    partner_scores(1)
    partner_scores(3)
    for slot in (LEFT, RIGHT):
        arrived(slot, VAL)
        arrived(slot, KEY)
    two = [one(r >= 2) for r in reach]
    some = [one(r >= 1) for r in reach]
    for b, pos, c in ((0, 0, 0), (0, 1, 1), (1, 0, 1)):
        place(b, pos, buf[LEFT, KEY, rows(c), :], buf[LEFT, VAL, rows(c), :])
    score(0, 0, 2, [two[0] * left_ok, some[0] * left_ok])
    score(1, 0, 1, [two[1] * left_ok])
    for b, pos, c in ((0, 4, 0), (1, 3, 0), (1, 4, 1)):
        place(b, pos, buf[RIGHT, KEY, rows(c), :], buf[RIGHT, VAL, rows(c), :])
    score(0, 4, 1, [two[0] * right_ok])
    score(1, 3, 2, [some[1] * right_ok, two[1] * right_ok])
    partner_scores(2)

    lane = lax.broadcasted_iota(jnp.int32, (BLOCK, BLOCK), 1)
    packed = jnp.zeros((BLOCK, BLOCK), F32)
    for b in range(2):

        def finish(h, packed, b=b):
            at_row = 2 * b + h
            e = e_s[at_row]
            inv_total = 1.0 / jnp.sum(e, axis=-1, keepdims=True)
            out = (dot_n(e.astype(BF16), vcat[b, :, head(h)]) * inv_total).astype(BF16)
            o_ref[rows(b), head(h)] = out
            delta = jnp.sum(
                g_ref[rows(b), head(h)].astype(F32) * out.astype(F32), axis=-1, keepdims=True
            )
            ds = (e * inv_total * (g_s[at_row] - delta)).astype(BF16)
            grad = dot_n(ds, kcat[b, :, head(h)]) * scale
            s = grad * gq_ref[pl.ds(h, 1), :]
            hat = qhat[rows(b), head(h)]
            first = jnp.mean(s, axis=-1, keepdims=True)
            second = jnp.mean(s * hat, axis=-1, keepdims=True)
            dq_ref[rows(b), head(h)] = (
                (s - first - hat * second) * qinv[rows(b), head(h)]
            ).astype(BF16)
            packed = jnp.where(lane == at_row, inv_total, packed)
            return jnp.where(lane == 4 + at_row, delta, packed)

        packed = lax.fori_loop(0, HEADS, finish, packed)
    stats = packed.T[:8]
    own_stat[...] = stats
    width = (1, BLOCK)
    for slot in range(SLOTS):
        out_stat[slot, 0:8, :] = stats
        for b in range(2):
            if slot in (LEFT, RIGHT):
                first, second = two[b], some[b]
            else:
                first = second = picks[b][slot - 2].astype(F32)
            out_stat[slot, 8 + b : 9 + b, :] = jnp.broadcast_to(first, width)
            out_stat[slot, 10 + b : 11 + b, :] = jnp.broadcast_to(second, width)
        out_stat[slot, 12:16, :] = jnp.zeros((4, BLOCK), F32)
    send(STAT)

    if relay:
        for what in (QRY, COT):
            arrived(near, what)
            each_forward(what, lambda c: c.start())

    dk_acc[...] = jnp.zeros(dk_acc.shape, F32)
    dv_acc[...] = jnp.zeros(dv_acc.shape, F32)

    def terms(key, val, qry, cot, inv_total, delta):
        p = jnp.exp2(dot_t(key, qry) * log2e_scale) * inv_total
        ds = (p * (dot_t(val, cot) - delta)).astype(BF16)
        return dot_n(ds, qry), dot_n(p.astype(BF16), cot)

    def band_terms(pairs, qry_of, cot_of, stat_of):
        def body(h, carry):
            for b, c, row in pairs:
                inv_total = stat_of(2 * b + h)
                if row is not None:
                    inv_total = inv_total * stat_of(row)
                dk, dv = terms(
                    kn[rows(c), head(h)],
                    v_ref[rows(c), head(h)],
                    qry_of(b, h),
                    cot_of(b, h),
                    inv_total,
                    stat_of(4 + 2 * b + h),
                )
                dk_acc[rows(c), head(h)] += dk
                dv_acc[rows(c), head(h)] += dv
            return carry

        lax.fori_loop(0, HEADS, body, 0)

    def own_body(h, carry):
        for b in range(2):
            for c in range(2):
                inv_total = own_stat[pl.ds(2 * b + h, 1), :]
                if b != c:
                    inv_total = inv_total * some[b]
                dk, dv = terms(
                    kn[rows(c), head(h)],
                    v_ref[rows(c), head(h)],
                    qn[rows(b), head(h)],
                    g_ref[rows(b), head(h)],
                    inv_total,
                    own_stat[pl.ds(4 + 2 * b + h, 1), :],
                )
                dk_acc[rows(c), head(h)] += dk
                dv_acc[rows(c), head(h)] += dv
        return carry

    lax.fori_loop(0, HEADS, own_body, 0)

    def partner_terms(level):
        slot = 2 + level
        if slot != near:
            arrived(slot, QRY)
            arrived(slot, COT)
        arrived(slot, STAT)

        def body(h, carry):
            for b in range(2):
                m = stat[slot, 8 + b : 9 + b, :]
                dk, dv = terms(
                    blend(m, kn[rows(0), head(h)], kn[rows(1), head(h)]),
                    blend(m, v_ref[rows(0), head(h)], v_ref[rows(1), head(h)]),
                    buf[slot, QRY, rows(b), head(h)],
                    buf[slot, COT, rows(b), head(h)],
                    stat[slot, pl.ds(2 * b + h, 1), :],
                    stat[slot, pl.ds(4 + 2 * b + h, 1), :],
                )
                dk_acc[rows(0), head(h)] += dk * (1.0 - m)
                dk_acc[rows(1), head(h)] += dk * m
                dv_acc[rows(0), head(h)] += dv * (1.0 - m)
                dv_acc[rows(1), head(h)] += dv * m
            return carry

        lax.fori_loop(0, HEADS, body, 0)

    partner_terms(0)
    partner_terms(1)
    partner_terms(3)
    for slot, pairs in (
        (LEFT, ((1, 0, 11), (0, 0, 8), (1, 1, 9))),
        (RIGHT, ((0, 1, 10), (0, 0, 8), (1, 1, 9))),
    ):
        for what in (QRY, COT, STAT):
            arrived(slot, what)
        band_terms(
            pairs,
            lambda b, h, slot=slot: buf[slot, QRY, rows(b), head(h)],
            lambda b, h, slot=slot: buf[slot, COT, rows(b), head(h)],
            lambda r, slot=slot: stat[slot, pl.ds(r, 1), :],
        )
    partner_terms(2)

    for h in range(HEADS):
        cols = slice(h * hd, (h + 1) * hd)
        s = dk_acc[:, cols] * (scale * gk_ref[h : h + 1, :])
        hat = khat[:, cols]
        first = jnp.mean(s, axis=-1, keepdims=True)
        second = jnp.mean(s * hat, axis=-1, keepdims=True)
        dk_ref[:, cols] = ((s - first - hat * second) * kinv[:, cols]).astype(BF16)
        dv_ref[:, cols] = dv_acc[:, cols].astype(BF16)

    for what in (VAL, KEY, QRY, COT, STAT):
        each_copy(what, lambda c: c.wait_send())
    for what in (VAL, KEY, QRY, COT):
        each_forward(what, lambda c: c.wait_send())


def solution(mesh):
    shards = mesh.shape["grp"] * mesh.shape["ctx"]
    inner = mesh.shape["ctx"]

    def body(query_raw, key_raw, values, band_reach, partners, gain_query, gain_key, cotangent):
        n, width = query_raw.shape
        cat = POS * BLOCK
        vmem = pl.BlockSpec(memory_space=pltpu.VMEM)
        smem = pl.BlockSpec(memory_space=pltpu.SMEM)
        out = jax.ShapeDtypeStruct((n, width), BF16)
        return pl.pallas_call(
            functools.partial(kernel, shards, inner),
            out_shape=(out,) * 4,
            in_specs=[vmem] * 6 + [smem] * 2,
            out_specs=(vmem,) * 4,
            scratch_shapes=[
                pltpu.VMEM((SLOTS, 4, n, width), BF16),
                pltpu.VMEM((SLOTS, 16, BLOCK), F32),
                pltpu.VMEM((8, BLOCK), F32),
                pltpu.VMEM((SLOTS, 16, BLOCK), F32),
                pltpu.VMEM((n, width), BF16),
                pltpu.VMEM((n, width), BF16),
                pltpu.VMEM((n, width), F32),
                pltpu.VMEM((n, width), F32),
                pltpu.VMEM((n, width), F32),
                pltpu.VMEM((n, width), F32),
                pltpu.VMEM((2, cat, width), BF16),
                pltpu.VMEM((2, cat, width), BF16),
                pltpu.VMEM((2 * HEADS, BLOCK, cat), F32),
                pltpu.VMEM((2 * HEADS, BLOCK, cat), F32),
                pltpu.VMEM((n, width), F32),
                pltpu.VMEM((n, width), F32),
                pltpu.SemaphoreType.DMA((SLOTS, 5)),
                pltpu.SemaphoreType.DMA((SLOTS, 5)),
                pltpu.SemaphoreType.DMA((4,)),
            ],
            compiler_params=pltpu.CompilerParams(
                collective_id=0, has_side_effects=True, vmem_limit_bytes=40 * 2**20
            ),
        )(query_raw, key_raw, values, cotangent, gain_query, gain_key, band_reach, partners)

    seq = P(AXES, None)
    return jax.shard_map(
        body,
        mesh=mesh,
        in_specs=(seq, seq, seq, P(AXES), seq, P(), P(), seq),
        out_specs=(seq,) * 4,
        check_vma=False,
    )
```

```python
import functools
import math

import jax
import jax.numpy as jnp
from jax import lax
from jax.experimental import pallas as pl
from jax.experimental.pallas import tpu as pltpu
from jax.sharding import PartitionSpec as P

HEADS = 2
BLOCK = 128
LEVELS = 4
BAND = 2
EPS = 1e-05
AXES = ("grp", "ctx")
MESH = pl.DeviceIdType.MESH
F32 = jnp.float32
BF16 = jnp.bfloat16
LEFT, RIGHT = 0, 1
SLOTS = 2 + LEVELS
KEY, VAL, QRY, COT, STAT = 0, 1, 2, 3, 4
POS = 2 * BAND + 1 + LEVELS


def dot_t(a, b):
    return lax.dot_general(a, b, (((1,), (1,)), ((), ())), preferred_element_type=F32)


def dot_n(a, b):
    return jnp.dot(a, b, preferred_element_type=F32)


def rows(block):
    return pl.ds(block * BLOCK, BLOCK)


def kernel(
    shards,
    inner,
    v_in,
    k_in,
    gk_in,
    q_in,
    gq_in,
    g_in,
    reach_in,
    part_in,
    o_out,
    dq_out,
    dk_out,
    dv_out,
    o_ref,
    dq_ref,
    dk_ref,
    dv_ref,
    v_ref,
    k_ref,
    gk_ref,
    q_ref,
    gq_ref,
    g_ref,
    reach_ref,
    part_ref,
    buf,
    stat,
    own_stat,
    out_stat,
    qn,
    kn,
    qhat,
    khat,
    qinv,
    kinv,
    kcat,
    vcat,
    e_s,
    g_s,
    dk_acc,
    dv_acc,
    send_sem,
    recv_sem,
    fwd_sem,
    far_sem,
    in_sem,
    out_sem,
):
    loads = [
        pltpu.make_async_copy(src, dst, in_sem.at[i])
        for i, (src, dst) in enumerate(
            (
                (v_in, v_ref),
                (k_in, k_ref),
                (gk_in, gk_ref),
                (q_in, q_ref),
                (gq_in, gq_ref),
                (g_in, g_ref),
                (reach_in, reach_ref),
                (part_in, part_ref),
            )
        )
    ]
    for load in loads:
        load.start()
    stores = [
        pltpu.make_async_copy(src, dst, out_sem.at[i])
        for i, (src, dst) in enumerate(
            ((o_ref, o_out), (dq_ref, dq_out), (dk_ref, dk_out), (dv_ref, dv_out))
        )
    ]
    me = lax.axis_index(AXES)
    hd = gq_ref.shape[1]
    scale = hd ** (-0.5)
    log2e_scale = scale * math.log2(math.e)
    masks = [shards >> (level + 1) for level in range(LEVELS)]
    relay = 2 in masks
    near = 2 + masks.index(2) if relay else None
    chain = relay and 4 in masks
    far = 2 + masks.index(4) if chain else None
    has_left = me > 0
    has_right = me < shards - 1
    core = lax.rem(me, 2)
    chip_odd = lax.rem(me // 2, 2)
    place_in_8 = lax.rem(me, 8)
    peers = [jnp.bitwise_xor(me, m) for m in masks]

    def at(t):
        return (t // inner, lax.rem(t, inner))

    barrier = pltpu.get_barrier_semaphore()
    for t in peers:
        pl.semaphore_signal(barrier, inc=1, device_id=at(t), device_id_type=MESH)

    @pl.when(has_left)
    def _():
        pl.semaphore_signal(barrier, inc=1, device_id=at(me - 1), device_id_type=MESH)

    @pl.when(has_right)
    def _():
        pl.semaphore_signal(barrier, inc=1, device_id=at(me + 1), device_id_type=MESH)

    if chain:

        @pl.when(place_in_8 == 3)
        def _():
            pl.semaphore_signal(barrier, inc=1, device_id=at(me - 3), device_id_type=MESH)

        @pl.when(place_in_8 == 0)
        def _():
            pl.semaphore_signal(barrier, inc=1, device_id=at(me + 3), device_id_type=MESH)

        @pl.when(place_in_8 == 4)
        def _():
            pl.semaphore_signal(barrier, inc=1, device_id=at(me + 3), device_id_type=MESH)

        @pl.when(place_in_8 == 7)
        def _():
            pl.semaphore_signal(barrier, inc=1, device_id=at(me - 3), device_id_type=MESH)

        extra = (
            (lax.rem(place_in_8, 4) == 0) | (lax.rem(place_in_8, 4) == 3)
        ).astype(jnp.int32)
    else:
        extra = 0
    pl.semaphore_wait(
        barrier, extra + LEVELS + has_left.astype(jnp.int32) + has_right.astype(jnp.int32)
    )

    sources = {KEY: kn, VAL: v_ref, QRY: qn, COT: g_ref}

    def copy(slot, what, t):
        if what == STAT:
            src, dst = out_stat.at[slot], stat.at[slot]
        else:
            src, dst = sources[what], buf.at[slot, what]
        return pltpu.make_async_remote_copy(
            src_ref=src,
            dst_ref=dst,
            send_sem=send_sem.at[slot, what],
            recv_sem=recv_sem.at[slot, what],
            device_id=at(t),
            device_id_type=MESH,
        )

    def forward(slot, what, t):
        return pltpu.make_async_remote_copy(
            src_ref=buf.at[near, what],
            dst_ref=buf.at[slot, what],
            send_sem=fwd_sem.at[what],
            recv_sem=recv_sem.at[slot, what],
            device_id=at(t),
            device_id_type=MESH,
        )

    def to_right(what):
        if relay and what != STAT:
            return has_right & ((core == 0) | (chip_odd == 1))
        return has_right

    def to_left(what):
        if relay and what != STAT:
            return has_left & ((core == 1) | (chip_odd == 0))
        return has_left

    def each_copy(what, act):
        @pl.when(to_right(what))
        def _():
            act(copy(LEFT, what, me + 1))

        @pl.when(to_left(what))
        def _():
            act(copy(RIGHT, what, me - 1))

        for level in reversed(range(LEVELS)):
            if 2 + level == far and what != STAT:

                @pl.when((place_in_8 != 3) & (place_in_8 != 4))
                def _(level=level):
                    act(copy(2 + level, what, peers[level]))
            else:
                act(copy(2 + level, what, peers[level]))

    def send(what):
        each_copy(what, lambda c: c.start())

    def arrived(slot, what):
        if slot == LEFT:

            @pl.when(has_left)
            def _():
                copy(LEFT, what, me - 1).wait_recv()
        elif slot == RIGHT:

            @pl.when(has_right)
            def _():
                copy(RIGHT, what, me + 1).wait_recv()
        else:
            copy(slot, what, peers[slot - 2]).wait_recv()

    def each_forward(what, act):
        if not relay:
            return

        @pl.when((core == 0) & (chip_odd == 0))
        def _():
            act(forward(RIGHT, what, me + 1))

        @pl.when((core == 1) & (chip_odd == 1))
        def _():
            act(forward(LEFT, what, me - 1))

    def chained(what, act):
        if not chain:
            return

        def hop(slot, t):
            return pltpu.make_async_remote_copy(
                src_ref=buf.at[slot, what],
                dst_ref=buf.at[far, what],
                send_sem=far_sem.at[what],
                recv_sem=recv_sem.at[far, what],
                device_id=at(t),
                device_id_type=MESH,
            )

        @pl.when(place_in_8 == 3)
        def _():
            act(hop(RIGHT, me - 3))

        @pl.when(place_in_8 == 4)
        def _():
            act(hop(LEFT, me + 3))

    def pass_on(what):
        if relay:
            arrived(near, what)
            each_forward(what, lambda c: c.start())
        arrived(LEFT, what)
        arrived(RIGHT, what)
        chained(what, lambda c: c.start())

    loads[0].wait()
    send(VAL)
    def normalize(x_ref, gain_ref, hat_ref, inv_ref, out_ref):
        for h in range(HEADS):
            cols = slice(h * hd, (h + 1) * hd)
            x = x_ref[:, cols].astype(F32)
            x = x - jnp.mean(x, axis=-1, keepdims=True)
            inv = lax.rsqrt(jnp.mean(x * x, axis=-1, keepdims=True) + EPS)
            hat = x * inv
            hat_ref[:, cols] = hat
            inv_ref[:, cols] = jnp.broadcast_to(inv, hat.shape)
            out_ref[:, cols] = (hat * gain_ref[h : h + 1, :]).astype(BF16)

    loads[1].wait()
    loads[2].wait()
    normalize(k_ref, gk_ref, khat, kinv, kn)
    send(KEY)
    loads[3].wait()
    loads[4].wait()
    normalize(q_ref, gq_ref, qhat, qinv, qn)
    send(QRY)
    loads[5].wait()
    send(COT)
    loads[6].wait()
    loads[7].wait()

    for slot, missing in ((LEFT, me == 0), (RIGHT, me == shards - 1)):

        @pl.when(missing)
        def _():
            for what in (KEY, VAL, QRY, COT):
                buf[slot, what] = jnp.zeros(buf.shape[2:], BF16)
            stat[slot] = jnp.zeros(stat.shape[1:], F32)

    def head(h):
        return pl.ds(pl.multiple_of(h * hd, hd), hd)

    reach = [reach_ref[b] for b in range(2)]
    picks = [[part_ref[b, lv] - peers[lv] * 2 for lv in range(LEVELS)] for b in range(2)]

    def one(flag):
        return jnp.where(flag, 1.0, 0.0).astype(F32)

    left_ok, right_ok = one(has_left), one(has_right)

    def score(b, first, count, weights):
        span = pl.ds(first * BLOCK, count * BLOCK)

        def body(h, carry):
            s = dot_t(qn[rows(b), head(h)], kcat[b, span, head(h)])
            gp = dot_t(g_ref[rows(b), head(h)], vcat[b, span, head(h)])
            e = jnp.exp2(s * log2e_scale)
            for i in range(count):
                w = weights[i]
                part = e[:, i * BLOCK : (i + 1) * BLOCK]
                if w is not None:
                    part = part * w
                e_s[2 * b + h, :, rows(first + i)] = part
            g_s[2 * b + h, :, span] = gp
            return carry

        lax.fori_loop(0, HEADS, body, 0)

    def place(b, pos, key, val):
        kcat[b, rows(pos), :] = key
        vcat[b, rows(pos), :] = val

    for b in range(2):
        for c in range(2):
            place(b, 2 - b + c, kn[rows(c), :], v_ref[rows(c), :])
        score(b, 2 - b, 2, [None if c == b else one(reach[b] >= 1) for c in range(2)])

    def blend(m, first, second):
        return (first.astype(F32) * (1.0 - m) + second.astype(F32) * m).astype(BF16)

    def partner_scores(level):
        slot = 2 + level
        if slot != near:
            arrived(slot, VAL)
            arrived(slot, KEY)
        for b in range(2):
            m = picks[b][level].astype(F32)
            place(
                b,
                2 * BAND + 1 + level,
                blend(m, buf[slot, KEY, rows(0), :], buf[slot, KEY, rows(1), :]),
                blend(m, buf[slot, VAL, rows(0), :], buf[slot, VAL, rows(1), :]),
            )
            score(b, 2 * BAND + 1 + level, 1, [None])

    partner_scores(0)
    partner_scores(1)
    pass_on(VAL)
    pass_on(KEY)
    partner_scores(3)
    two = [one(r >= 2) for r in reach]
    some = [one(r >= 1) for r in reach]
    for b, pos, c in ((0, 0, 0), (0, 1, 1), (1, 0, 1)):
        place(b, pos, buf[LEFT, KEY, rows(c), :], buf[LEFT, VAL, rows(c), :])
    score(0, 0, 2, [two[0] * left_ok, some[0] * left_ok])
    score(1, 0, 1, [two[1] * left_ok])
    for b, pos, c in ((0, 4, 0), (1, 3, 0), (1, 4, 1)):
        place(b, pos, buf[RIGHT, KEY, rows(c), :], buf[RIGHT, VAL, rows(c), :])
    score(0, 4, 1, [two[0] * right_ok])
    score(1, 3, 2, [some[1] * right_ok, two[1] * right_ok])
    partner_scores(2)

    lane = lax.broadcasted_iota(jnp.int32, (BLOCK, BLOCK), 1)
    packed = jnp.zeros((BLOCK, BLOCK), F32)
    for b in range(2):

        def finish(h, packed, b=b):
            at_row = 2 * b + h
            e = e_s[at_row]
            inv_total = 1.0 / jnp.sum(e, axis=-1, keepdims=True)
            out = (dot_n(e.astype(BF16), vcat[b, :, head(h)]) * inv_total).astype(BF16)
            o_ref[rows(b), head(h)] = out
            delta = jnp.sum(
                g_ref[rows(b), head(h)].astype(F32) * out.astype(F32), axis=-1, keepdims=True
            )
            ds = (e * inv_total * (g_s[at_row] - delta)).astype(BF16)
            grad = dot_n(ds, kcat[b, :, head(h)]) * scale
            s = grad * gq_ref[pl.ds(h, 1), :]
            hat = qhat[rows(b), head(h)]
            first = jnp.mean(s, axis=-1, keepdims=True)
            second = jnp.mean(s * hat, axis=-1, keepdims=True)
            dq_ref[rows(b), head(h)] = (
                (s - first - hat * second) * qinv[rows(b), head(h)]
            ).astype(BF16)
            packed = jnp.where(lane == at_row, inv_total, packed)
            return jnp.where(lane == 4 + at_row, delta, packed)

        packed = lax.fori_loop(0, HEADS, finish, packed)
    stats = packed.T[:8]
    own_stat[...] = stats
    width = (1, BLOCK)
    for slot in range(SLOTS):
        out_stat[slot, 0:8, :] = stats
        for b in range(2):
            if slot in (LEFT, RIGHT):
                first, second = two[b], some[b]
            else:
                first = second = picks[b][slot - 2].astype(F32)
            out_stat[slot, 8 + b : 9 + b, :] = jnp.broadcast_to(first, width)
            out_stat[slot, 10 + b : 11 + b, :] = jnp.broadcast_to(second, width)
        out_stat[slot, 12:16, :] = jnp.zeros((4, BLOCK), F32)
    send(STAT)
    stores[0].start()
    stores[1].start()

    pass_on(QRY)

    dk_acc[...] = jnp.zeros(dk_acc.shape, F32)
    dv_acc[...] = jnp.zeros(dv_acc.shape, F32)

    def terms(key, val, qry, cot, inv_total, delta):
        p = jnp.exp2(dot_t(key, qry) * log2e_scale) * inv_total
        ds = (p * (dot_t(val, cot) - delta)).astype(BF16)
        return dot_n(ds, qry), dot_n(p.astype(BF16), cot)

    def band_terms(pairs, qry_of, cot_of, stat_of):
        def body(h, carry):
            for b, c, row in pairs:
                inv_total = stat_of(2 * b + h)
                if row is not None:
                    inv_total = inv_total * stat_of(row)
                dk, dv = terms(
                    kn[rows(c), head(h)],
                    v_ref[rows(c), head(h)],
                    qry_of(b, h),
                    cot_of(b, h),
                    inv_total,
                    stat_of(4 + 2 * b + h),
                )
                dk_acc[rows(c), head(h)] += dk
                dv_acc[rows(c), head(h)] += dv
            return carry

        lax.fori_loop(0, HEADS, body, 0)

    def own_body(h, carry):
        for b in range(2):
            for c in range(2):
                inv_total = own_stat[pl.ds(2 * b + h, 1), :]
                if b != c:
                    inv_total = inv_total * some[b]
                dk, dv = terms(
                    kn[rows(c), head(h)],
                    v_ref[rows(c), head(h)],
                    qn[rows(b), head(h)],
                    g_ref[rows(b), head(h)],
                    inv_total,
                    own_stat[pl.ds(4 + 2 * b + h, 1), :],
                )
                dk_acc[rows(c), head(h)] += dk
                dv_acc[rows(c), head(h)] += dv
        return carry

    lax.fori_loop(0, HEADS, own_body, 0)

    def partner_terms(level):
        slot = 2 + level
        if slot != near:
            arrived(slot, QRY)
            arrived(slot, COT)
        arrived(slot, STAT)

        def body(h, carry):
            for b in range(2):
                m = stat[slot, 8 + b : 9 + b, :]
                dk, dv = terms(
                    blend(m, kn[rows(0), head(h)], kn[rows(1), head(h)]),
                    blend(m, v_ref[rows(0), head(h)], v_ref[rows(1), head(h)]),
                    buf[slot, QRY, rows(b), head(h)],
                    buf[slot, COT, rows(b), head(h)],
                    stat[slot, pl.ds(2 * b + h, 1), :],
                    stat[slot, pl.ds(4 + 2 * b + h, 1), :],
                )
                dk_acc[rows(0), head(h)] += dk * (1.0 - m)
                dk_acc[rows(1), head(h)] += dk * m
                dv_acc[rows(0), head(h)] += dv * (1.0 - m)
                dv_acc[rows(1), head(h)] += dv * m
            return carry

        lax.fori_loop(0, HEADS, body, 0)

    partner_terms(0)
    partner_terms(1)
    pass_on(COT)
    partner_terms(3)
    for slot, pairs in (
        (LEFT, ((1, 0, 11), (0, 0, 8), (1, 1, 9))),
        (RIGHT, ((0, 1, 10), (0, 0, 8), (1, 1, 9))),
    ):
        arrived(slot, STAT)
        band_terms(
            pairs,
            lambda b, h, slot=slot: buf[slot, QRY, rows(b), head(h)],
            lambda b, h, slot=slot: buf[slot, COT, rows(b), head(h)],
            lambda r, slot=slot: stat[slot, pl.ds(r, 1), :],
        )
    partner_terms(2)

    dv_ref[...] = dv_acc[...].astype(BF16)
    stores[3].start()
    for h in range(HEADS):
        cols = slice(h * hd, (h + 1) * hd)
        s = dk_acc[:, cols] * (scale * gk_ref[h : h + 1, :])
        hat = khat[:, cols]
        first = jnp.mean(s, axis=-1, keepdims=True)
        second = jnp.mean(s * hat, axis=-1, keepdims=True)
        dk_ref[:, cols] = ((s - first - hat * second) * kinv[:, cols]).astype(BF16)
    stores[2].start()

    for what in (VAL, KEY, QRY, COT, STAT):
        each_copy(what, lambda c: c.wait_send())
    for what in (VAL, KEY, QRY, COT):
        each_forward(what, lambda c: c.wait_send())
        chained(what, lambda c: c.wait_send())
    for store in stores:
        store.wait()


def hand_on(*refs):
    count = (len(refs) - 2) // 3
    in_sem, out_sem = refs[-2:]
    held = refs[2 * count : 3 * count]
    loads = [pltpu.make_async_copy(refs[i], held[i], in_sem.at[i]) for i in range(count)]
    stores = [
        pltpu.make_async_copy(held[i], refs[count + i], out_sem.at[i]) for i in range(count)
    ]
    for c in loads:
        c.start()
    for load, store in zip(loads, stores):
        load.wait()
        store.start()
    for c in stores:
        c.wait()


def solution(mesh):
    shards = mesh.shape["grp"] * mesh.shape["ctx"]
    inner = mesh.shape["ctx"]

    def body(query_raw, key_raw, values, band_reach, partners, gain_query, gain_key, cotangent):
        n, width = query_raw.shape
        cat = POS * BLOCK
        hbm = pl.BlockSpec(memory_space=pltpu.HBM)
        out = jax.ShapeDtypeStruct((n, width), BF16)
        results = pl.pallas_call(
            functools.partial(kernel, shards, inner),
            out_shape=(out,) * 4,
            in_specs=[hbm] * 8,
            out_specs=(hbm,) * 4,
            scratch_shapes=[
                pltpu.VMEM((n, width), BF16),
                pltpu.VMEM((n, width), BF16),
                pltpu.VMEM((n, width), BF16),
                pltpu.VMEM((n, width), BF16),
                pltpu.VMEM((n, width), BF16),
                pltpu.VMEM((n, width), BF16),
                pltpu.VMEM(gain_key.shape, F32),
                pltpu.VMEM((n, width), BF16),
                pltpu.VMEM(gain_query.shape, F32),
                pltpu.VMEM((n, width), BF16),
                pltpu.SMEM(band_reach.shape, jnp.int32),
                pltpu.SMEM(partners.shape, jnp.int32),
                pltpu.VMEM((SLOTS, 4, n, width), BF16),
                pltpu.VMEM((SLOTS, 16, BLOCK), F32),
                pltpu.VMEM((8, BLOCK), F32),
                pltpu.VMEM((SLOTS, 16, BLOCK), F32),
                pltpu.VMEM((n, width), BF16),
                pltpu.VMEM((n, width), BF16),
                pltpu.VMEM((n, width), F32),
                pltpu.VMEM((n, width), F32),
                pltpu.VMEM((n, width), F32),
                pltpu.VMEM((n, width), F32),
                pltpu.VMEM((2, cat, width), BF16),
                pltpu.VMEM((2, cat, width), BF16),
                pltpu.VMEM((2 * HEADS, BLOCK, cat), F32),
                pltpu.VMEM((2 * HEADS, BLOCK, cat), F32),
                pltpu.VMEM((n, width), F32),
                pltpu.VMEM((n, width), F32),
                pltpu.SemaphoreType.DMA((SLOTS, 5)),
                pltpu.SemaphoreType.DMA((SLOTS, 5)),
                pltpu.SemaphoreType.DMA((4,)),
                pltpu.SemaphoreType.DMA((4,)),
                pltpu.SemaphoreType.DMA((8,)),
                pltpu.SemaphoreType.DMA((4,)),
            ],
            compiler_params=pltpu.CompilerParams(
                collective_id=0, has_side_effects=True, vmem_limit_bytes=64 * 2**20
            ),
        )(values, key_raw, gain_key, query_raw, gain_query, cotangent, band_reach, partners)
        return pl.pallas_call(
            hand_on,
            out_shape=(out,) * 4,
            in_specs=[hbm] * 4,
            out_specs=(hbm,) * 4,
            scratch_shapes=[pltpu.VMEM((n, width), BF16)] * 4
            + [pltpu.SemaphoreType.DMA((4,))] * 2,
        )(*results)

    seq = P(AXES, None)
    return jax.shard_map(
        body,
        mesh=mesh,
        in_specs=(seq, seq, seq, P(AXES), seq, P(), P(), seq),
        out_specs=(seq,) * 4,
        check_vma=False,
    )
```

```python
import functools
import math

import jax
import jax.numpy as jnp
from jax import lax
from jax.experimental import pallas as pl
from jax.experimental.pallas import tpu as pltpu
from jax.sharding import PartitionSpec as P

HEADS = 2
BLOCK = 128
LEVELS = 4
BAND = 2
EPS = 1e-05
AXES = ("grp", "ctx")
MESH = pl.DeviceIdType.MESH
F32 = jnp.float32
BF16 = jnp.bfloat16
LEFT, RIGHT = 0, 1
SLOTS = 2 + LEVELS
KEY, VAL, QRY, COT, STAT = 0, 1, 2, 3, 4
POS = 2 * BAND + 1 + LEVELS
RELAYED = (KEY, VAL, QRY, COT)
CHAINED = (KEY, VAL, QRY, COT)


def dot_t(a, b):
    return lax.dot_general(a, b, (((1,), (1,)), ((), ())), preferred_element_type=F32)


def dot_n(a, b):
    return jnp.dot(a, b, preferred_element_type=F32)


def rows(block):
    return pl.ds(block * BLOCK, BLOCK)


def kernel(
    shards,
    inner,
    v_in,
    k_in,
    gk_in,
    q_in,
    gq_in,
    g_in,
    reach_in,
    part_in,
    o_out,
    dq_out,
    dk_out,
    dv_out,
    o_ref,
    dq_ref,
    dk_ref,
    dv_ref,
    v_ref,
    k_ref,
    gk_ref,
    q_ref,
    gq_ref,
    g_ref,
    reach_ref,
    part_ref,
    buf,
    stat,
    own_stat,
    out_stat,
    qn,
    kn,
    qhat,
    khat,
    qinv,
    kinv,
    kcat,
    vcat,
    e_s,
    g_s,
    dk_acc,
    dv_acc,
    send_sem,
    recv_sem,
    fwd_sem,
    far_sem,
    in_sem,
    out_sem,
):
    loads = [
        pltpu.make_async_copy(src, dst, in_sem.at[i])
        for i, (src, dst) in enumerate(
            (
                (v_in, v_ref),
                (k_in, k_ref),
                (gk_in, gk_ref),
                (q_in, q_ref),
                (gq_in, gq_ref),
                (g_in, g_ref),
                (reach_in, reach_ref),
                (part_in, part_ref),
            )
        )
    ]
    for load in loads:
        load.start()
    stores = [
        pltpu.make_async_copy(src, dst, out_sem.at[i])
        for i, (src, dst) in enumerate(
            ((o_ref, o_out), (dq_ref, dq_out), (dk_ref, dk_out), (dv_ref, dv_out))
        )
    ]
    me = lax.axis_index(AXES)
    hd = gq_ref.shape[1]
    scale = hd ** (-0.5)
    log2e_scale = scale * math.log2(math.e)
    masks = [shards >> (level + 1) for level in range(LEVELS)]
    relay = 2 in masks
    near = 2 + masks.index(2) if relay else None
    chain = relay and 4 in masks
    far = 2 + masks.index(4) if chain else None
    has_left = me > 0
    has_right = me < shards - 1
    core = lax.rem(me, 2)
    chip_odd = lax.rem(me // 2, 2)
    place_in_8 = lax.rem(me, 8)
    peers = [jnp.bitwise_xor(me, m) for m in masks]

    def at(t):
        return (t // inner, lax.rem(t, inner))

    barrier = pltpu.get_barrier_semaphore()
    for t in peers:
        pl.semaphore_signal(barrier, inc=1, device_id=at(t), device_id_type=MESH)

    @pl.when(has_left)
    def _():
        pl.semaphore_signal(barrier, inc=1, device_id=at(me - 1), device_id_type=MESH)

    @pl.when(has_right)
    def _():
        pl.semaphore_signal(barrier, inc=1, device_id=at(me + 1), device_id_type=MESH)

    if chain:

        @pl.when(place_in_8 == 3)
        def _():
            pl.semaphore_signal(barrier, inc=1, device_id=at(me - 3), device_id_type=MESH)

        @pl.when(place_in_8 == 0)
        def _():
            pl.semaphore_signal(barrier, inc=1, device_id=at(me + 3), device_id_type=MESH)

        @pl.when(place_in_8 == 4)
        def _():
            pl.semaphore_signal(barrier, inc=1, device_id=at(me + 3), device_id_type=MESH)

        @pl.when(place_in_8 == 7)
        def _():
            pl.semaphore_signal(barrier, inc=1, device_id=at(me - 3), device_id_type=MESH)

        extra = (
            (lax.rem(place_in_8, 4) == 0) | (lax.rem(place_in_8, 4) == 3)
        ).astype(jnp.int32)
    else:
        extra = 0
    pl.semaphore_wait(
        barrier, extra + LEVELS + has_left.astype(jnp.int32) + has_right.astype(jnp.int32)
    )

    sources = {KEY: kn, VAL: v_ref, QRY: qn, COT: g_ref}

    def copy(slot, what, t):
        if what == STAT:
            src, dst = out_stat.at[slot], stat.at[slot]
        else:
            src, dst = sources[what], buf.at[slot, what]
        return pltpu.make_async_remote_copy(
            src_ref=src,
            dst_ref=dst,
            send_sem=send_sem.at[slot, what],
            recv_sem=recv_sem.at[slot, what],
            device_id=at(t),
            device_id_type=MESH,
        )

    def forward(slot, what, t):
        return pltpu.make_async_remote_copy(
            src_ref=buf.at[near, what],
            dst_ref=buf.at[slot, what],
            send_sem=fwd_sem.at[what],
            recv_sem=recv_sem.at[slot, what],
            device_id=at(t),
            device_id_type=MESH,
        )

    def to_right(what):
        if relay and what in RELAYED:
            return has_right & ((core == 0) | (chip_odd == 1))
        return has_right

    def to_left(what):
        if relay and what in RELAYED:
            return has_left & ((core == 1) | (chip_odd == 0))
        return has_left

    def each_copy(what, act):
        @pl.when(to_right(what))
        def _():
            act(copy(LEFT, what, me + 1))

        @pl.when(to_left(what))
        def _():
            act(copy(RIGHT, what, me - 1))

        for level in reversed(range(LEVELS)):
            if 2 + level == far and what in CHAINED:

                @pl.when((place_in_8 != 3) & (place_in_8 != 4))
                def _(level=level):
                    act(copy(2 + level, what, peers[level]))
            else:
                act(copy(2 + level, what, peers[level]))

    def send(what):
        each_copy(what, lambda c: c.start())

    def arrived(slot, what):
        if slot == LEFT:

            @pl.when(has_left)
            def _():
                copy(LEFT, what, me - 1).wait_recv()
        elif slot == RIGHT:

            @pl.when(has_right)
            def _():
                copy(RIGHT, what, me + 1).wait_recv()
        else:
            copy(slot, what, peers[slot - 2]).wait_recv()

    def each_forward(what, act):
        if not relay or what not in RELAYED:
            return

        @pl.when((core == 0) & (chip_odd == 0))
        def _():
            act(forward(RIGHT, what, me + 1))

        @pl.when((core == 1) & (chip_odd == 1))
        def _():
            act(forward(LEFT, what, me - 1))

    def chained(what, act):
        if not chain or what not in CHAINED:
            return

        def hop(slot, t):
            return pltpu.make_async_remote_copy(
                src_ref=buf.at[slot, what],
                dst_ref=buf.at[far, what],
                send_sem=far_sem.at[what],
                recv_sem=recv_sem.at[far, what],
                device_id=at(t),
                device_id_type=MESH,
            )

        @pl.when(place_in_8 == 3)
        def _():
            act(hop(RIGHT, me - 3))

        @pl.when(place_in_8 == 4)
        def _():
            act(hop(LEFT, me + 3))

    def pass_near(what):
        if relay:
            arrived(near, what)
            each_forward(what, lambda c: c.start())

    def pass_far(what):
        arrived(LEFT, what)
        arrived(RIGHT, what)
        chained(what, lambda c: c.start())

    loads[0].wait()
    send(VAL)
    def normalize(x_ref, gain_ref, hat_ref, inv_ref, out_ref):
        for h in range(HEADS):
            cols = slice(h * hd, (h + 1) * hd)
            x = x_ref[:, cols].astype(F32)
            x = x - jnp.mean(x, axis=-1, keepdims=True)
            inv = lax.rsqrt(jnp.mean(x * x, axis=-1, keepdims=True) + EPS)
            hat = x * inv
            hat_ref[:, cols] = hat
            inv_ref[:, cols] = jnp.broadcast_to(inv, hat.shape)
            out_ref[:, cols] = (hat * gain_ref[h : h + 1, :]).astype(BF16)

    loads[1].wait()
    loads[2].wait()
    normalize(k_ref, gk_ref, khat, kinv, kn)
    send(KEY)
    loads[3].wait()
    loads[4].wait()
    normalize(q_ref, gq_ref, qhat, qinv, qn)
    send(QRY)
    loads[5].wait()
    send(COT)
    loads[6].wait()
    loads[7].wait()

    for slot, missing in ((LEFT, me == 0), (RIGHT, me == shards - 1)):

        @pl.when(missing)
        def _():
            for what in (KEY, VAL, QRY, COT):
                buf[slot, what] = jnp.zeros(buf.shape[2:], BF16)
            stat[slot] = jnp.zeros(stat.shape[1:], F32)

    def head(h):
        return pl.ds(pl.multiple_of(h * hd, hd), hd)

    reach = [reach_ref[b] for b in range(2)]
    picks = [[part_ref[b, lv] - peers[lv] * 2 for lv in range(LEVELS)] for b in range(2)]

    def one(flag):
        return jnp.where(flag, 1.0, 0.0).astype(F32)

    left_ok, right_ok = one(has_left), one(has_right)

    def score(b, first, count, weights):
        span = pl.ds(first * BLOCK, count * BLOCK)

        def body(h, carry):
            s = dot_t(qn[rows(b), head(h)], kcat[b, span, head(h)])
            gp = dot_t(g_ref[rows(b), head(h)], vcat[b, span, head(h)])
            e = jnp.exp2(s * log2e_scale)
            for i in range(count):
                w = weights[i]
                part = e[:, i * BLOCK : (i + 1) * BLOCK]
                if w is not None:
                    part = part * w
                e_s[2 * b + h, :, rows(first + i)] = part
            g_s[2 * b + h, :, span] = gp
            return carry

        lax.fori_loop(0, HEADS, body, 0, unroll=True)

    def place(b, pos, key, val):
        kcat[b, rows(pos), :] = key
        vcat[b, rows(pos), :] = val

    for b in range(2):
        for c in range(2):
            place(b, 2 - b + c, kn[rows(c), :], v_ref[rows(c), :])
        score(b, 2 - b, 2, [None if c == b else one(reach[b] >= 1) for c in range(2)])

    def blend(m, first, second):
        return (first.astype(F32) * (1.0 - m) + second.astype(F32) * m).astype(BF16)

    def partner_scores(level):
        slot = 2 + level
        if slot != near:
            arrived(slot, VAL)
            arrived(slot, KEY)
        for b in range(2):
            m = picks[b][level].astype(F32)
            place(
                b,
                2 * BAND + 1 + level,
                blend(m, buf[slot, KEY, rows(0), :], buf[slot, KEY, rows(1), :]),
                blend(m, buf[slot, VAL, rows(0), :], buf[slot, VAL, rows(1), :]),
            )
            score(b, 2 * BAND + 1 + level, 1, [None])

    pass_near(VAL)
    partner_scores(0)
    pass_far(VAL)
    pass_near(KEY)
    partner_scores(1)
    pass_far(KEY)
    partner_scores(3)
    two = [one(r >= 2) for r in reach]
    some = [one(r >= 1) for r in reach]
    for b, pos, c in ((0, 0, 0), (0, 1, 1), (1, 0, 1)):
        place(b, pos, buf[LEFT, KEY, rows(c), :], buf[LEFT, VAL, rows(c), :])
    score(0, 0, 2, [two[0] * left_ok, some[0] * left_ok])
    score(1, 0, 1, [two[1] * left_ok])
    for b, pos, c in ((0, 4, 0), (1, 3, 0), (1, 4, 1)):
        place(b, pos, buf[RIGHT, KEY, rows(c), :], buf[RIGHT, VAL, rows(c), :])
    score(0, 4, 1, [two[0] * right_ok])
    score(1, 3, 2, [some[1] * right_ok, two[1] * right_ok])
    partner_scores(2)

    lane = lax.broadcasted_iota(jnp.int32, (BLOCK, BLOCK), 1)
    packed = jnp.zeros((BLOCK, BLOCK), F32)
    for b in range(2):

        def finish(h, packed, b=b):
            at_row = 2 * b + h
            e = e_s[at_row]
            inv_total = 1.0 / jnp.sum(e, axis=-1, keepdims=True)
            out = (dot_n(e.astype(BF16), vcat[b, :, head(h)]) * inv_total).astype(BF16)
            o_ref[rows(b), head(h)] = out
            delta = jnp.sum(
                g_ref[rows(b), head(h)].astype(F32) * out.astype(F32), axis=-1, keepdims=True
            )
            ds = (e * inv_total * (g_s[at_row] - delta)).astype(BF16)
            grad = dot_n(ds, kcat[b, :, head(h)]) * scale
            s = grad * gq_ref[pl.ds(h, 1), :]
            hat = qhat[rows(b), head(h)]
            first = jnp.mean(s, axis=-1, keepdims=True)
            second = jnp.mean(s * hat, axis=-1, keepdims=True)
            dq_ref[rows(b), head(h)] = (
                (s - first - hat * second) * qinv[rows(b), head(h)]
            ).astype(BF16)
            packed = jnp.where(lane == at_row, inv_total, packed)
            return jnp.where(lane == 4 + at_row, delta, packed)

        packed = lax.fori_loop(0, HEADS, finish, packed, unroll=True)
    stats = packed.T[:8]
    own_stat[...] = stats
    width = (1, BLOCK)
    for slot in range(SLOTS):
        out_stat[slot, 0:8, :] = stats
        for b in range(2):
            if slot in (LEFT, RIGHT):
                first, second = two[b], some[b]
            else:
                first = second = picks[b][slot - 2].astype(F32)
            out_stat[slot, 8 + b : 9 + b, :] = jnp.broadcast_to(first, width)
            out_stat[slot, 10 + b : 11 + b, :] = jnp.broadcast_to(second, width)
        out_stat[slot, 12:16, :] = jnp.zeros((4, BLOCK), F32)
    send(STAT)
    stores[0].start()
    stores[1].start()


    dk_acc[...] = jnp.zeros(dk_acc.shape, F32)
    dv_acc[...] = jnp.zeros(dv_acc.shape, F32)

    def terms(key, val, qry, cot, inv_total, delta):
        p = jnp.exp2(dot_t(key, qry) * log2e_scale) * inv_total
        ds = (p * (dot_t(val, cot) - delta)).astype(BF16)
        return dot_n(ds, qry), dot_n(p.astype(BF16), cot)

    def band_terms(pairs, qry_of, cot_of, stat_of):
        def body(h, carry):
            for b, c, row in pairs:
                inv_total = stat_of(2 * b + h)
                if row is not None:
                    inv_total = inv_total * stat_of(row)
                dk, dv = terms(
                    kn[rows(c), head(h)],
                    v_ref[rows(c), head(h)],
                    qry_of(b, h),
                    cot_of(b, h),
                    inv_total,
                    stat_of(4 + 2 * b + h),
                )
                dk_acc[rows(c), head(h)] += dk
                dv_acc[rows(c), head(h)] += dv
            return carry

        lax.fori_loop(0, HEADS, body, 0, unroll=True)

    def own_body(h, carry):
        for b in range(2):
            for c in range(2):
                inv_total = own_stat[pl.ds(2 * b + h, 1), :]
                if b != c:
                    inv_total = inv_total * some[b]
                dk, dv = terms(
                    kn[rows(c), head(h)],
                    v_ref[rows(c), head(h)],
                    qn[rows(b), head(h)],
                    g_ref[rows(b), head(h)],
                    inv_total,
                    own_stat[pl.ds(4 + 2 * b + h, 1), :],
                )
                dk_acc[rows(c), head(h)] += dk
                dv_acc[rows(c), head(h)] += dv
        return carry

    lax.fori_loop(0, HEADS, own_body, 0, unroll=True)

    def partner_terms(level):
        slot = 2 + level
        if slot != near:
            arrived(slot, QRY)
            arrived(slot, COT)
        arrived(slot, STAT)

        def body(h, carry):
            for b in range(2):
                m = stat[slot, 8 + b : 9 + b, :]
                dk, dv = terms(
                    blend(m, kn[rows(0), head(h)], kn[rows(1), head(h)]),
                    blend(m, v_ref[rows(0), head(h)], v_ref[rows(1), head(h)]),
                    buf[slot, QRY, rows(b), head(h)],
                    buf[slot, COT, rows(b), head(h)],
                    stat[slot, pl.ds(2 * b + h, 1), :],
                    stat[slot, pl.ds(4 + 2 * b + h, 1), :],
                )
                dk_acc[rows(0), head(h)] += dk * (1.0 - m)
                dk_acc[rows(1), head(h)] += dk * m
                dv_acc[rows(0), head(h)] += dv * (1.0 - m)
                dv_acc[rows(1), head(h)] += dv * m
            return carry

        lax.fori_loop(0, HEADS, body, 0, unroll=True)

    pass_near(QRY)
    pass_far(QRY)
    partner_terms(0)
    partner_terms(1)
    pass_near(COT)
    pass_far(COT)
    partner_terms(3)
    for slot, pairs in (
        (LEFT, ((1, 0, 11), (0, 0, 8), (1, 1, 9))),
        (RIGHT, ((0, 1, 10), (0, 0, 8), (1, 1, 9))),
    ):
        arrived(slot, STAT)
        band_terms(
            pairs,
            lambda b, h, slot=slot: buf[slot, QRY, rows(b), head(h)],
            lambda b, h, slot=slot: buf[slot, COT, rows(b), head(h)],
            lambda r, slot=slot: stat[slot, pl.ds(r, 1), :],
        )
    partner_terms(2)

    dv_ref[...] = dv_acc[...].astype(BF16)
    stores[3].start()
    for h in range(HEADS):
        cols = slice(h * hd, (h + 1) * hd)
        s = dk_acc[:, cols] * (scale * gk_ref[h : h + 1, :])
        hat = khat[:, cols]
        first = jnp.mean(s, axis=-1, keepdims=True)
        second = jnp.mean(s * hat, axis=-1, keepdims=True)
        dk_ref[:, cols] = ((s - first - hat * second) * kinv[:, cols]).astype(BF16)
    stores[2].start()

    for what in (VAL, KEY, QRY, COT, STAT):
        each_copy(what, lambda c: c.wait_send())
    for what in (VAL, KEY, QRY, COT):
        each_forward(what, lambda c: c.wait_send())
        chained(what, lambda c: c.wait_send())
    for store in stores:
        store.wait()


def hand_on(*refs):
    count = (len(refs) - 2) // 3
    in_sem, out_sem = refs[-2:]
    held = refs[2 * count : 3 * count]
    loads = [pltpu.make_async_copy(refs[i], held[i], in_sem.at[i]) for i in range(count)]
    stores = [
        pltpu.make_async_copy(held[i], refs[count + i], out_sem.at[i]) for i in range(count)
    ]
    for c in loads:
        c.start()
    for load, store in zip(loads, stores):
        load.wait()
        store.start()
    for c in stores:
        c.wait()


def solution(mesh):
    shards = mesh.shape["grp"] * mesh.shape["ctx"]
    inner = mesh.shape["ctx"]

    def body(query_raw, key_raw, values, band_reach, partners, gain_query, gain_key, cotangent):
        n, width = query_raw.shape
        cat = POS * BLOCK
        hbm = pl.BlockSpec(memory_space=pltpu.HBM)
        out = jax.ShapeDtypeStruct((n, width), BF16)
        results = pl.pallas_call(
            functools.partial(kernel, shards, inner),
            out_shape=(out,) * 4,
            in_specs=[hbm] * 8,
            out_specs=(hbm,) * 4,
            scratch_shapes=[
                pltpu.VMEM((n, width), BF16),
                pltpu.VMEM((n, width), BF16),
                pltpu.VMEM((n, width), BF16),
                pltpu.VMEM((n, width), BF16),
                pltpu.VMEM((n, width), BF16),
                pltpu.VMEM((n, width), BF16),
                pltpu.VMEM(gain_key.shape, F32),
                pltpu.VMEM((n, width), BF16),
                pltpu.VMEM(gain_query.shape, F32),
                pltpu.VMEM((n, width), BF16),
                pltpu.SMEM(band_reach.shape, jnp.int32),
                pltpu.SMEM(partners.shape, jnp.int32),
                pltpu.VMEM((SLOTS, 4, n, width), BF16),
                pltpu.VMEM((SLOTS, 16, BLOCK), F32),
                pltpu.VMEM((8, BLOCK), F32),
                pltpu.VMEM((SLOTS, 16, BLOCK), F32),
                pltpu.VMEM((n, width), BF16),
                pltpu.VMEM((n, width), BF16),
                pltpu.VMEM((n, width), F32),
                pltpu.VMEM((n, width), F32),
                pltpu.VMEM((n, width), F32),
                pltpu.VMEM((n, width), F32),
                pltpu.VMEM((2, cat, width), BF16),
                pltpu.VMEM((2, cat, width), BF16),
                pltpu.VMEM((2 * HEADS, BLOCK, cat), F32),
                pltpu.VMEM((2 * HEADS, BLOCK, cat), F32),
                pltpu.VMEM((n, width), F32),
                pltpu.VMEM((n, width), F32),
                pltpu.SemaphoreType.DMA((SLOTS, 5)),
                pltpu.SemaphoreType.DMA((SLOTS, 5)),
                pltpu.SemaphoreType.DMA((4,)),
                pltpu.SemaphoreType.DMA((4,)),
                pltpu.SemaphoreType.DMA((8,)),
                pltpu.SemaphoreType.DMA((4,)),
            ],
            compiler_params=pltpu.CompilerParams(
                collective_id=0, has_side_effects=True, vmem_limit_bytes=64 * 2**20
            ),
        )(values, key_raw, gain_key, query_raw, gain_query, cotangent, band_reach, partners)
        return pl.pallas_call(
            hand_on,
            out_shape=(out,) * 4,
            in_specs=[hbm] * 4,
            out_specs=(hbm,) * 4,
            scratch_shapes=[pltpu.VMEM((n, width), BF16)] * 4
            + [pltpu.SemaphoreType.DMA((4,))] * 2,
        )(*results)

    seq = P(AXES, None)
    return jax.shard_map(
        body,
        mesh=mesh,
        in_specs=(seq, seq, seq, P(AXES), seq, P(), P(), seq),
        out_specs=(seq,) * 4,
        check_vma=False,
    )
```

```python
import functools
import math

import jax
import jax.numpy as jnp
from jax import lax
from jax.experimental import pallas as pl
from jax.experimental.pallas import tpu as pltpu
from jax.sharding import PartitionSpec as P

HEADS = 2
BLOCK = 128
LEVELS = 4
BAND = 2
EPS = 1e-05
AXES = ("grp", "ctx")
MESH = pl.DeviceIdType.MESH
F32 = jnp.float32
BF16 = jnp.bfloat16
LEFT, RIGHT = 0, 1
SLOTS = 2 + LEVELS
KEY, VAL, QRY, COT, STAT = 0, 1, 2, 3, 4
POS = 2 * BAND + 1 + LEVELS
RELAYED = (KEY, VAL, QRY, COT)
CHAINED = (KEY, VAL, QRY, COT)


def dot_t(a, b):
    return lax.dot_general(a, b, (((1,), (1,)), ((), ())), preferred_element_type=F32)


def dot_n(a, b):
    return jnp.dot(a, b, preferred_element_type=F32)


def rows(block):
    return pl.ds(block * BLOCK, BLOCK)


def kernel(
    shards,
    inner,
    v_in,
    k_in,
    gk_in,
    q_in,
    gq_in,
    g_in,
    reach_in,
    part_in,
    o_out,
    dq_out,
    dk_out,
    dv_out,
    o_ref,
    dq_ref,
    dk_ref,
    dv_ref,
    v_ref,
    k_ref,
    gk_ref,
    q_ref,
    gq_ref,
    g_ref,
    reach_ref,
    part_ref,
    buf,
    stat,
    own_stat,
    out_stat,
    qn,
    kn,
    qhat,
    khat,
    qinv,
    kinv,
    kcat,
    vcat,
    e_s,
    g_s,
    dk_acc,
    dv_acc,
    ahead_s,
    partner_s,
    send_sem,
    recv_sem,
    fwd_sem,
    far_sem,
    in_sem,
    out_sem,
):
    loads = [
        pltpu.make_async_copy(src, dst, in_sem.at[i])
        for i, (src, dst) in enumerate(
            (
                (v_in, v_ref),
                (k_in, k_ref),
                (gk_in, gk_ref),
                (q_in, q_ref),
                (gq_in, gq_ref),
                (g_in, g_ref),
                (reach_in, reach_ref),
                (part_in, part_ref),
            )
        )
    ]
    for load in loads:
        load.start()
    stores = [
        pltpu.make_async_copy(src, dst, out_sem.at[i])
        for i, (src, dst) in enumerate(
            ((o_ref, o_out), (dq_ref, dq_out), (dk_ref, dk_out), (dv_ref, dv_out))
        )
    ]
    me = lax.axis_index(AXES)
    hd = gq_ref.shape[1]
    scale = hd ** (-0.5)
    log2e_scale = scale * math.log2(math.e)
    masks = [shards >> (level + 1) for level in range(LEVELS)]
    relay = 2 in masks
    near = 2 + masks.index(2) if relay else None
    chain = relay and 4 in masks
    far = 2 + masks.index(4) if chain else None
    has_left = me > 0
    has_right = me < shards - 1
    core = lax.rem(me, 2)
    chip_odd = lax.rem(me // 2, 2)
    place_in_8 = lax.rem(me, 8)
    peers = [jnp.bitwise_xor(me, m) for m in masks]

    def at(t):
        return (t // inner, lax.rem(t, inner))

    barrier = pltpu.get_barrier_semaphore()
    for t in peers:
        pl.semaphore_signal(barrier, inc=1, device_id=at(t), device_id_type=MESH)

    @pl.when(has_left)
    def _():
        pl.semaphore_signal(barrier, inc=1, device_id=at(me - 1), device_id_type=MESH)

    @pl.when(has_right)
    def _():
        pl.semaphore_signal(barrier, inc=1, device_id=at(me + 1), device_id_type=MESH)

    if chain:

        @pl.when(place_in_8 == 3)
        def _():
            pl.semaphore_signal(barrier, inc=1, device_id=at(me - 3), device_id_type=MESH)

        @pl.when(place_in_8 == 0)
        def _():
            pl.semaphore_signal(barrier, inc=1, device_id=at(me + 3), device_id_type=MESH)

        @pl.when(place_in_8 == 4)
        def _():
            pl.semaphore_signal(barrier, inc=1, device_id=at(me + 3), device_id_type=MESH)

        @pl.when(place_in_8 == 7)
        def _():
            pl.semaphore_signal(barrier, inc=1, device_id=at(me - 3), device_id_type=MESH)

        extra = (
            (lax.rem(place_in_8, 4) == 0) | (lax.rem(place_in_8, 4) == 3)
        ).astype(jnp.int32)
    else:
        extra = 0
    pl.semaphore_wait(
        barrier, extra + LEVELS + has_left.astype(jnp.int32) + has_right.astype(jnp.int32)
    )

    sources = {KEY: kn, VAL: v_ref, QRY: qn, COT: g_ref}

    def copy(slot, what, t):
        if what == STAT:
            src, dst = out_stat.at[slot], stat.at[slot]
        else:
            src, dst = sources[what], buf.at[slot, what]
        return pltpu.make_async_remote_copy(
            src_ref=src,
            dst_ref=dst,
            send_sem=send_sem.at[slot, what],
            recv_sem=recv_sem.at[slot, what],
            device_id=at(t),
            device_id_type=MESH,
        )

    def forward(slot, what, t):
        return pltpu.make_async_remote_copy(
            src_ref=buf.at[near, what],
            dst_ref=buf.at[slot, what],
            send_sem=fwd_sem.at[what],
            recv_sem=recv_sem.at[slot, what],
            device_id=at(t),
            device_id_type=MESH,
        )

    def to_right(what):
        if relay and what in RELAYED:
            return has_right & ((core == 0) | (chip_odd == 1))
        return has_right

    def to_left(what):
        if relay and what in RELAYED:
            return has_left & ((core == 1) | (chip_odd == 0))
        return has_left

    def each_copy(what, act):
        @pl.when(to_right(what))
        def _():
            act(copy(LEFT, what, me + 1))

        @pl.when(to_left(what))
        def _():
            act(copy(RIGHT, what, me - 1))

        for level in reversed(range(LEVELS)):
            if 2 + level == far and what in CHAINED:

                @pl.when((place_in_8 != 3) & (place_in_8 != 4))
                def _(level=level):
                    act(copy(2 + level, what, peers[level]))
            else:
                act(copy(2 + level, what, peers[level]))

    def send(what):
        each_copy(what, lambda c: c.start())

    def arrived(slot, what):
        if slot == LEFT:

            @pl.when(has_left)
            def _():
                copy(LEFT, what, me - 1).wait_recv()
        elif slot == RIGHT:

            @pl.when(has_right)
            def _():
                copy(RIGHT, what, me + 1).wait_recv()
        else:
            copy(slot, what, peers[slot - 2]).wait_recv()

    def each_forward(what, act):
        if not relay or what not in RELAYED:
            return

        @pl.when((core == 0) & (chip_odd == 0))
        def _():
            act(forward(RIGHT, what, me + 1))

        @pl.when((core == 1) & (chip_odd == 1))
        def _():
            act(forward(LEFT, what, me - 1))

    def chained(what, act):
        if not chain or what not in CHAINED:
            return

        def hop(slot, t):
            return pltpu.make_async_remote_copy(
                src_ref=buf.at[slot, what],
                dst_ref=buf.at[far, what],
                send_sem=far_sem.at[what],
                recv_sem=recv_sem.at[far, what],
                device_id=at(t),
                device_id_type=MESH,
            )

        @pl.when(place_in_8 == 3)
        def _():
            act(hop(RIGHT, me - 3))

        @pl.when(place_in_8 == 4)
        def _():
            act(hop(LEFT, me + 3))

    def pass_near(what):
        if relay:
            arrived(near, what)
            each_forward(what, lambda c: c.start())

    def pass_far(what):
        arrived(LEFT, what)
        arrived(RIGHT, what)
        chained(what, lambda c: c.start())

    loads[0].wait()
    send(VAL)
    def normalize(x_ref, gain_ref, hat_ref, inv_ref, out_ref):
        for h in range(HEADS):
            cols = slice(h * hd, (h + 1) * hd)
            x = x_ref[:, cols].astype(F32)
            x = x - jnp.mean(x, axis=-1, keepdims=True)
            inv = lax.rsqrt(jnp.mean(x * x, axis=-1, keepdims=True) + EPS)
            hat = x * inv
            hat_ref[:, cols] = hat
            inv_ref[:, cols] = jnp.broadcast_to(inv, hat.shape)
            out_ref[:, cols] = (hat * gain_ref[h : h + 1, :]).astype(BF16)

    loads[1].wait()
    loads[2].wait()
    normalize(k_ref, gk_ref, khat, kinv, kn)
    send(KEY)
    loads[3].wait()
    loads[4].wait()
    normalize(q_ref, gq_ref, qhat, qinv, qn)
    send(QRY)
    loads[5].wait()
    send(COT)
    loads[6].wait()
    loads[7].wait()

    for slot, missing in ((LEFT, me == 0), (RIGHT, me == shards - 1)):

        @pl.when(missing)
        def _():
            for what in (KEY, VAL, QRY, COT):
                buf[slot, what] = jnp.zeros(buf.shape[2:], BF16)
            stat[slot] = jnp.zeros(stat.shape[1:], F32)

    def head(h):
        return pl.ds(pl.multiple_of(h * hd, hd), hd)

    reach = [reach_ref[b] for b in range(2)]
    picks = [[part_ref[b, lv] - peers[lv] * 2 for lv in range(LEVELS)] for b in range(2)]

    def one(flag):
        return jnp.where(flag, 1.0, 0.0).astype(F32)

    left_ok, right_ok = one(has_left), one(has_right)

    def score(b, first, count, weights):
        span = pl.ds(first * BLOCK, count * BLOCK)

        def body(h, carry):
            s = dot_t(qn[rows(b), head(h)], kcat[b, span, head(h)])
            gp = dot_t(g_ref[rows(b), head(h)], vcat[b, span, head(h)])
            e = jnp.exp2(s * log2e_scale)
            for i in range(count):
                w = weights[i]
                part = e[:, i * BLOCK : (i + 1) * BLOCK]
                if w is not None:
                    part = part * w
                e_s[2 * b + h, :, rows(first + i)] = part
            g_s[2 * b + h, :, span] = gp
            return carry

        lax.fori_loop(0, HEADS, body, 0, unroll=True)

    def place(b, pos, key, val):
        kcat[b, rows(pos), :] = key
        vcat[b, rows(pos), :] = val

    for b in range(2):
        for c in range(2):
            place(b, 2 - b + c, kn[rows(c), :], v_ref[rows(c), :])
        score(b, 2 - b, 2, [None if c == b else one(reach[b] >= 1) for c in range(2)])

    def blend(m, first, second):
        return (first.astype(F32) * (1.0 - m) + second.astype(F32) * m).astype(BF16)

    def partner_scores(level):
        slot = 2 + level
        if slot != near:
            arrived(slot, VAL)
            arrived(slot, KEY)
        for b in range(2):
            m = picks[b][level].astype(F32)
            place(
                b,
                2 * BAND + 1 + level,
                blend(m, buf[slot, KEY, rows(0), :], buf[slot, KEY, rows(1), :]),
                blend(m, buf[slot, VAL, rows(0), :], buf[slot, VAL, rows(1), :]),
            )
            score(b, 2 * BAND + 1 + level, 1, [None])

    pass_near(VAL)
    partner_scores(0)
    pass_far(VAL)
    pass_near(KEY)
    partner_scores(1)
    pass_far(KEY)
    partner_scores(3)
    two = [one(r >= 2) for r in reach]
    some = [one(r >= 1) for r in reach]
    for b, pos, c in ((0, 0, 0), (0, 1, 1), (1, 0, 1)):
        place(b, pos, buf[LEFT, KEY, rows(c), :], buf[LEFT, VAL, rows(c), :])
    score(0, 0, 2, [two[0] * left_ok, some[0] * left_ok])
    score(1, 0, 1, [two[1] * left_ok])
    for b, pos, c in ((0, 4, 0), (1, 3, 0), (1, 4, 1)):
        place(b, pos, buf[RIGHT, KEY, rows(c), :], buf[RIGHT, VAL, rows(c), :])
    score(0, 4, 1, [two[0] * right_ok])
    score(1, 3, 2, [some[1] * right_ok, two[1] * right_ok])
    partner_scores(2)

    lane = lax.broadcasted_iota(jnp.int32, (BLOCK, BLOCK), 1)
    packed = jnp.zeros((BLOCK, BLOCK), F32)
    for b in range(2):

        def finish(h, packed, b=b):
            at_row = 2 * b + h
            e = e_s[at_row]
            inv_total = 1.0 / jnp.sum(e, axis=-1, keepdims=True)
            out = (dot_n(e.astype(BF16), vcat[b, :, head(h)]) * inv_total).astype(BF16)
            o_ref[rows(b), head(h)] = out
            delta = jnp.sum(
                g_ref[rows(b), head(h)].astype(F32) * out.astype(F32), axis=-1, keepdims=True
            )
            ds = (e * inv_total * (g_s[at_row] - delta)).astype(BF16)
            grad = dot_n(ds, kcat[b, :, head(h)]) * scale
            s = grad * gq_ref[pl.ds(h, 1), :]
            hat = qhat[rows(b), head(h)]
            first = jnp.mean(s, axis=-1, keepdims=True)
            second = jnp.mean(s * hat, axis=-1, keepdims=True)
            dq_ref[rows(b), head(h)] = (
                (s - first - hat * second) * qinv[rows(b), head(h)]
            ).astype(BF16)
            packed = jnp.where(lane == at_row, inv_total, packed)
            return jnp.where(lane == 4 + at_row, delta, packed)

        packed = lax.fori_loop(0, HEADS, finish, packed, unroll=True)
    stats = packed.T[:8]
    own_stat[...] = stats
    width = (1, BLOCK)
    for slot in range(SLOTS):
        out_stat[slot, 0:8, :] = stats
        for b in range(2):
            if slot in (LEFT, RIGHT):
                first, second = two[b], some[b]
            else:
                first = second = picks[b][slot - 2].astype(F32)
            out_stat[slot, 8 + b : 9 + b, :] = jnp.broadcast_to(first, width)
            out_stat[slot, 10 + b : 11 + b, :] = jnp.broadcast_to(second, width)
        out_stat[slot, 12:16, :] = jnp.zeros((4, BLOCK), F32)
    send(STAT)
    stores[0].start()
    stores[1].start()


    dk_acc[...] = jnp.zeros(dk_acc.shape, F32)
    dv_acc[...] = jnp.zeros(dv_acc.shape, F32)

    def terms(key, val, qry, cot, inv_total, delta, e=None):
        if e is None:
            e = jnp.exp2(dot_t(key, qry) * log2e_scale)
        p = e * inv_total
        ds = (p * (dot_t(val, cot) - delta)).astype(BF16)
        return dot_n(ds, qry), dot_n(p.astype(BF16), cot)

    def ahead(slot, pairs):
        for h in range(HEADS):
            cols = slice(h * hd, (h + 1) * hd)
            for i, (b, c, _) in enumerate(pairs):
                s = dot_t(kn[rows(c), cols], buf[slot, QRY, rows(b), cols])
                ahead_s[slot, i, h] = jnp.exp2(s * log2e_scale)

    def band_terms(slot, pairs, qry_of, cot_of, stat_of):
        def body(h, carry):
            for i, (b, c, row) in enumerate(pairs):
                inv_total = stat_of(2 * b + h)
                if row is not None:
                    inv_total = inv_total * stat_of(row)
                dk, dv = terms(
                    kn[rows(c), head(h)],
                    v_ref[rows(c), head(h)],
                    qry_of(b, h),
                    cot_of(b, h),
                    inv_total,
                    stat_of(4 + 2 * b + h),
                    ahead_s[slot, i, h],
                )
                dk_acc[rows(c), head(h)] += dk
                dv_acc[rows(c), head(h)] += dv
            return carry

        lax.fori_loop(0, HEADS, body, 0, unroll=True)

    def own_body(h, carry):
        for b in range(2):
            for c in range(2):
                inv_total = own_stat[pl.ds(2 * b + h, 1), :]
                if b != c:
                    inv_total = inv_total * some[b]
                dk, dv = terms(
                    kn[rows(c), head(h)],
                    v_ref[rows(c), head(h)],
                    qn[rows(b), head(h)],
                    g_ref[rows(b), head(h)],
                    inv_total,
                    own_stat[pl.ds(4 + 2 * b + h, 1), :],
                )
                dk_acc[rows(c), head(h)] += dk
                dv_acc[rows(c), head(h)] += dv
        return carry

    lax.fori_loop(0, HEADS, own_body, 0, unroll=True)

    def partner_ahead(level):
        slot = 2 + level
        if slot != near:
            arrived(slot, QRY)
        arrived(slot, STAT)
        for h in range(HEADS):
            cols = slice(h * hd, (h + 1) * hd)
            for b in range(2):
                m = stat[slot, 8 + b : 9 + b, :]
                key = blend(m, kn[rows(0), cols], kn[rows(1), cols])
                s = dot_t(key, buf[slot, QRY, rows(b), cols])
                partner_s[level - 2, b, h] = jnp.exp2(s * log2e_scale)

    def partner_terms(level):
        slot = 2 + level
        if level < 2:
            arrived(slot, QRY)
            arrived(slot, STAT)
        if slot != near:
            arrived(slot, COT)

        def body(h, carry):
            for b in range(2):
                m = stat[slot, 8 + b : 9 + b, :]
                dk, dv = terms(
                    blend(m, kn[rows(0), head(h)], kn[rows(1), head(h)]),
                    blend(m, v_ref[rows(0), head(h)], v_ref[rows(1), head(h)]),
                    buf[slot, QRY, rows(b), head(h)],
                    buf[slot, COT, rows(b), head(h)],
                    stat[slot, pl.ds(2 * b + h, 1), :],
                    stat[slot, pl.ds(4 + 2 * b + h, 1), :],
                    partner_s[level - 2, b, h] if level >= 2 else None,
                )
                dk_acc[rows(0), head(h)] += dk * (1.0 - m)
                dk_acc[rows(1), head(h)] += dk * m
                dv_acc[rows(0), head(h)] += dv * (1.0 - m)
                dv_acc[rows(1), head(h)] += dv * m
            return carry

        lax.fori_loop(0, HEADS, body, 0, unroll=True)

    pass_near(QRY)
    pass_far(QRY)
    partner_terms(0)
    partner_terms(1)
    band_pairs = (
        (LEFT, ((1, 0, 11), (0, 0, 8), (1, 1, 9))),
        (RIGHT, ((0, 1, 10), (0, 0, 8), (1, 1, 9))),
    )
    for slot, pairs in band_pairs:
        ahead(slot, pairs)
    partner_ahead(3)
    partner_ahead(2)
    pass_near(COT)
    pass_far(COT)
    partner_terms(3)
    for slot, pairs in band_pairs:
        arrived(slot, STAT)
        band_terms(
            slot,
            pairs,
            lambda b, h, slot=slot: buf[slot, QRY, rows(b), head(h)],
            lambda b, h, slot=slot: buf[slot, COT, rows(b), head(h)],
            lambda r, slot=slot: stat[slot, pl.ds(r, 1), :],
        )
    partner_terms(2)

    dv_ref[...] = dv_acc[...].astype(BF16)
    stores[3].start()
    for h in range(HEADS):
        cols = slice(h * hd, (h + 1) * hd)
        s = dk_acc[:, cols] * (scale * gk_ref[h : h + 1, :])
        hat = khat[:, cols]
        first = jnp.mean(s, axis=-1, keepdims=True)
        second = jnp.mean(s * hat, axis=-1, keepdims=True)
        dk_ref[:, cols] = ((s - first - hat * second) * kinv[:, cols]).astype(BF16)
    stores[2].start()

    for what in (VAL, KEY, QRY, COT, STAT):
        each_copy(what, lambda c: c.wait_send())
    for what in (VAL, KEY, QRY, COT):
        each_forward(what, lambda c: c.wait_send())
        chained(what, lambda c: c.wait_send())
    for store in stores:
        store.wait()


def hand_on(*refs):
    count = (len(refs) - 2) // 3
    in_sem, out_sem = refs[-2:]
    held = refs[2 * count : 3 * count]
    loads = [pltpu.make_async_copy(refs[i], held[i], in_sem.at[i]) for i in range(count)]
    stores = [
        pltpu.make_async_copy(held[i], refs[count + i], out_sem.at[i]) for i in range(count)
    ]
    for c in loads:
        c.start()
    for load, store in zip(loads, stores):
        load.wait()
        store.start()
    for c in stores:
        c.wait()


def solution(mesh):
    shards = mesh.shape["grp"] * mesh.shape["ctx"]
    inner = mesh.shape["ctx"]

    def body(query_raw, key_raw, values, band_reach, partners, gain_query, gain_key, cotangent):
        n, width = query_raw.shape
        cat = POS * BLOCK
        hbm = pl.BlockSpec(memory_space=pltpu.HBM)
        out = jax.ShapeDtypeStruct((n, width), BF16)
        results = pl.pallas_call(
            functools.partial(kernel, shards, inner),
            out_shape=(out,) * 4,
            in_specs=[hbm] * 8,
            out_specs=(hbm,) * 4,
            scratch_shapes=[
                pltpu.VMEM((n, width), BF16),
                pltpu.VMEM((n, width), BF16),
                pltpu.VMEM((n, width), BF16),
                pltpu.VMEM((n, width), BF16),
                pltpu.VMEM((n, width), BF16),
                pltpu.VMEM((n, width), BF16),
                pltpu.VMEM(gain_key.shape, F32),
                pltpu.VMEM((n, width), BF16),
                pltpu.VMEM(gain_query.shape, F32),
                pltpu.VMEM((n, width), BF16),
                pltpu.SMEM(band_reach.shape, jnp.int32),
                pltpu.SMEM(partners.shape, jnp.int32),
                pltpu.VMEM((SLOTS, 4, n, width), BF16),
                pltpu.VMEM((SLOTS, 16, BLOCK), F32),
                pltpu.VMEM((8, BLOCK), F32),
                pltpu.VMEM((SLOTS, 16, BLOCK), F32),
                pltpu.VMEM((n, width), BF16),
                pltpu.VMEM((n, width), BF16),
                pltpu.VMEM((n, width), F32),
                pltpu.VMEM((n, width), F32),
                pltpu.VMEM((n, width), F32),
                pltpu.VMEM((n, width), F32),
                pltpu.VMEM((2, cat, width), BF16),
                pltpu.VMEM((2, cat, width), BF16),
                pltpu.VMEM((2 * HEADS, BLOCK, cat), F32),
                pltpu.VMEM((2 * HEADS, BLOCK, cat), F32),
                pltpu.VMEM((n, width), F32),
                pltpu.VMEM((n, width), F32),
                pltpu.VMEM((2, 3, HEADS, BLOCK, BLOCK), F32),
                pltpu.VMEM((2, 2, HEADS, BLOCK, BLOCK), F32),
                pltpu.SemaphoreType.DMA((SLOTS, 5)),
                pltpu.SemaphoreType.DMA((SLOTS, 5)),
                pltpu.SemaphoreType.DMA((4,)),
                pltpu.SemaphoreType.DMA((4,)),
                pltpu.SemaphoreType.DMA((8,)),
                pltpu.SemaphoreType.DMA((4,)),
            ],
            compiler_params=pltpu.CompilerParams(
                collective_id=0, has_side_effects=True, vmem_limit_bytes=64 * 2**20
            ),
        )(values, key_raw, gain_key, query_raw, gain_query, cotangent, band_reach, partners)
        return pl.pallas_call(
            hand_on,
            out_shape=(out,) * 4,
            in_specs=[hbm] * 4,
            out_specs=(hbm,) * 4,
            scratch_shapes=[pltpu.VMEM((n, width), BF16)] * 4
            + [pltpu.SemaphoreType.DMA((4,))] * 2,
        )(*results)

    seq = P(AXES, None)
    return jax.shard_map(
        body,
        mesh=mesh,
        in_specs=(seq, seq, seq, P(AXES), seq, P(), P(), seq),
        out_specs=(seq,) * 4,
        check_vma=False,
    )
```
